128 devices in a mesh: pb: 16 (over z, y), pa: 8 (over x, core).
Axes of the slice: x: 4, y: 4, z: 4, core: 2. Of those that a mesh axis runs over, the one named last changes fastest.
Arguments:
- hidden_in: bfloat16 [32768, 2048], P(('pb', 'pa')), may hold values from -6 to 6
- norm_gain: float32 [2048], replicated, may hold values from 0.1 to 1.9
- query_weight: bfloat16 [2048, 2048], replicated, may hold values from -0.125 to 0.125
- out_weight: bfloat16 [2048, 2048], replicated, may hold values from -0.125 to 0.125
- corpus_kv: bfloat16 [128, 64, 4096], P('pb'), may hold values from -24 to 24
- owner_ids: int32 [16, 8, 8, 2, 1], P('pb', 'pa'), may hold values from 0 to 15; in each aligned block of 16 rows (0 to 15, 16 to 31, ..., all dimensions but the last counted through in order) at most 2 rows name the same one
- local_ids: int32 [16, 8, 8, 2], P('pb', 'pa'), may hold values from 0 to 7
- counts: int32 [128], P('pb'), may hold values from 1 to 16
Outputs:
- update: bfloat16 [32768, 2048], P(('pb', 'pa'))
The draws below stay inside these ranges and needn't reach their ends.
Inputs may be any that keep to these rules, and one draw needn't show every extreme that they name: `owner_ids`: among the 16 slots of one device (one entry [b, p]), no corpus shard is named more than 2 times, a bound that some block reaches.
All inputs are finite; a program needn't handle non-finite values.
Results may differ from the reference program's by a relative error of at most 0.011.
The reference program's roundings to bfloat16 on the way (of `normed`, `queries`, `rounded` and `attended`) count: a program that leaves them out, or rounds other values in their place, can miss the bound.
Values may be sent and summed in bfloat16 or wider, within the bound.
No kernel may reach another device: no remote copies, remote signals or barrier semaphores. Data moves between devices by JAX's collectives and lax.ppermute only.
A program may use at most 320 MiB of HBM per device.

```python
import math
import jax
import jax.numpy as jnp
import numpy as np
from jax import lax

D = 2048
H = 32
DH = 64
Q_GRP = 8
SLOTS = 16
P_SIZE = 64
TQ = 256
PASS_DEV = 8
QUESTIONS = 128
ROWS = 32768
SL_DEV = 2
MOST = 2
CORPUS = 128
N_PB = 16
N_PA = 8


def draw_corpus_kv(key, part):
    key = jax.random.fold_in(key, 7)
    base = jax.random.normal(jax.random.fold_in(key, 1), (CORPUS, P_SIZE, 2 * D), jnp.float32)
    column = jnp.arange(2 * D)
    scale = jnp.where(column < D, 0.3, 1.0)[None, None, :]
    return jnp.clip(base * scale, -24.0, 24.0).astype(jnp.bfloat16)


def place_ends(result, rng, smallest, largest):
    longest = result.shape.index(max(result.shape))
    spots = []
    for shift in (0, 1):
        where = [jax.random.randint(jax.random.fold_in(rng, axis), (), 0, length) for axis, length in enumerate(result.shape)]
        where[longest] = (where[longest] + shift) % result.shape[longest]
        spots.append(tuple(where))
    return result.at[spots[0]].set(smallest).at[spots[1]].set(largest)


def steps_of(rng, dims, cuts, smallest, largest):
    gain, own = 1.0, jax.random.fold_in(rng, 6)
    for axis_at, blocks in cuts:
        draws = jnp.exp(jax.random.uniform(jax.random.fold_in(own, axis_at), (blocks,), jnp.float32, smallest / len(cuts), largest / len(cuts)))
        gain = gain * jnp.repeat(draws, dims[axis_at] // blocks).reshape([-1 if axis == axis_at else 1 for axis in range(len(dims))])
    return gain


def deal_out(key, own, number, rows, number_of, top, limit, skew):
    sequence = jax.random.permutation(key, number_of)
    packed, usual = load_shares(number_of, rows * top, limit, skew, True), load_shares(number_of, rows * top, limit, skew, False)
    places = jnp.arange(number_of)

    def named(sizes, offset_by):
        used = int((sizes > 0).sum())
        fixed = max(1, used // 4)
        moved = fixed + (places - fixed + offset_by * (used - fixed)) % max(1, number_of - fixed)
        return jnp.zeros((number_of,), jnp.int32).at[sequence[jnp.where(places < fixed, places, moved)]].set(jnp.asarray(sizes, jnp.int32))

    sizes = jnp.where(number % 4 == 0, named(packed, number // 4), named(usual, number - number // 4 - 1))
    mixed = jax.random.permutation(jax.random.fold_in(own, 3), number_of)
    source_of, sink = mixed[0:number_of // 2 * 2:2], mixed[1:number_of // 2 * 2:2]
    room = jnp.minimum(sizes[source_of] - 1, limit - sizes[sink]) // 2
    room = jnp.where((source_of == sequence[0]) | (sink == sequence[0]) | (sizes[sink] == 0), 0, jnp.maximum(room, 0))
    moved = jax.random.randint(jax.random.fold_in(own, 4), (number_of // 2,), 0, 1 << 20) % (room + 1)
    sizes = sizes.at[source_of].add(-moved).at[sink].add(moved)
    labels = jnp.searchsorted(jnp.cumsum(sizes), jnp.arange(rows * top), side="right").astype(jnp.int32)
    table = labels.reshape(top, rows).T
    table = table[jax.random.permutation(jax.random.fold_in(own, 1), rows)]
    offset_by = jax.random.randint(jax.random.fold_in(own, 2), (rows, 1), 0, top)
    return jnp.take_along_axis(table, (jnp.arange(top)[None, :] + offset_by) % top, axis=1)


def load_shares(count, total, bound, lean, full):
    loads = [(1 << 20) // math.isqrt(grade ** lean) + 1 for grade in range(1, count + 1)]
    largest = bound if full else min(bound, max(-(-total // count), total * loads[0] // sum(loads)))
    least = 1 if total - largest >= count - 1 else 0
    given, surplus = [largest] + [least] * (count - 1), total - largest - least * (count - 1)
    while surplus > 0:
        candidates = [i for i in range(1, count) if given[i] < largest] or [i for i in range(1, count) if given[i] < bound]
        mass, budget = sum([loads[i] for i in candidates]), surplus
        for i in candidates:
            extra = min(bound - given[i], max(1, budget * loads[i] // mass), surplus)
            given[i] = given[i] + extra
            surplus = surplus - extra
    return np.array(given)


def centred(own_key, shape, deviation, most, pieces=(), kind=jnp.bfloat16):
    entries = deviation * jax.random.normal(own_key, shape, jnp.float32)
    if pieces:
        entries = entries * steps_of(own_key, shape, pieces, -0.22, 0.18)
    return jnp.clip(entries, -most, most).astype(kind)


def setup_inputs(seed: int = 0) -> dict:
    keys = jax.random.split(jax.random.key(seed), 9)
    hidden_in = centred(keys[0], (ROWS, D), 1.0, 6.0, ((0, 128),))
    norm_gain = jnp.clip(1.0 + 0.18 * jax.random.normal(keys[1], (D,), jnp.float32), 0.1, 1.9)
    query_weight = centred(keys[2], (D, D), D ** -0.5, 0.125)
    out_weight = centred(keys[3], (D, D), D ** -0.5, 0.125)
    corpus_kv = draw_corpus_kv(jax.random.fold_in(keys[8], 71), 0)
    owner_ids_keys = jax.random.split(jax.random.fold_in(keys[5], 1), N_PB * N_PA * Q_GRP * SL_DEV // (Q_GRP * SL_DEV))
    owner_ids_turns = jax.random.permutation(jax.random.fold_in(keys[5], 3), N_PB * N_PA * Q_GRP * SL_DEV // (Q_GRP * SL_DEV))
    owner_ids = jax.vmap(lambda own, number: deal_out(jax.random.fold_in(keys[5], 2), own, number, Q_GRP * SL_DEV, N_PB, 1, MOST, 1))(owner_ids_keys, owner_ids_turns).reshape((N_PB, N_PA, Q_GRP, SL_DEV, 1))
    local_ids = place_ends(jax.random.randint(keys[6], (N_PB, N_PA, Q_GRP, SL_DEV), 0, PASS_DEV), jax.random.fold_in(keys[6], 1), 0, PASS_DEV - 1).astype(jnp.int32)
    counts = place_ends(jax.random.randint(keys[7], (QUESTIONS,), 1, SLOTS + 1), jax.random.fold_in(keys[7], 1), 1, SLOTS).astype(jnp.int32)
    return {"hidden_in": hidden_in, "norm_gain": norm_gain, "query_weight": query_weight, "out_weight": out_weight, "corpus_kv": corpus_kv, "owner_ids": owner_ids, "local_ids": local_ids, "counts": counts}


def scaled_norm(hidden_in, norm_gain):
    widened = hidden_in.astype(jnp.float32)
    factor = lax.rsqrt(lax.optimization_barrier(jnp.mean(widened * widened, axis=-1, keepdims=True)) + 1e-06)
    return (widened * factor * norm_gain).astype(jnp.bfloat16)

def reference(hidden_in, norm_gain, query_weight, out_weight, corpus_kv, owner_ids, local_ids, counts):
    normed = scaled_norm(hidden_in, norm_gain)
    queries = jnp.dot(normed, query_weight, preferred_element_type=jnp.float32).astype(jnp.bfloat16)
    passage_ids = owner_ids[..., 0] * PASS_DEV + local_ids
    passage_ids = jnp.transpose(passage_ids, (0, 2, 1, 3)).reshape(QUESTIONS, SLOTS).astype(jnp.int32)
    live_slots = jnp.arange(SLOTS, dtype=jnp.int32)[None, :] < counts[:, None]
    query_rows = queries.reshape(QUESTIONS, TQ, H, DH)

    def per_question(inputs):
        query_block, id_block, live_block = inputs
        stored = corpus_kv[id_block]
        key_rows = stored[:, :, :D].reshape(SLOTS * P_SIZE, H, DH).astype(jnp.float32)
        value_rows = stored[:, :, D:].reshape(SLOTS * P_SIZE, H, DH).astype(jnp.float32)
        live_keys = jnp.repeat(live_block, P_SIZE)
        scores = jnp.einsum('thd,khd->htk', query_block.astype(jnp.float32), key_rows)
        scores = jnp.where(live_keys[None, None, :], scores, -1e+30)
        row_top = lax.optimization_barrier(jnp.max(scores, axis=-1, keepdims=True))
        exp_scores = jnp.where(live_keys[None, None, :], jnp.exp(scores - row_top), 0.0)
        totals = lax.optimization_barrier(jnp.sum(exp_scores, axis=-1))
        rounded = lax.optimization_barrier(exp_scores.astype(jnp.bfloat16))
        numerators = jnp.einsum('htk,khd->thd', rounded.astype(jnp.float32), value_rows)
        outputs = numerators / jnp.transpose(totals)[:, :, None]
        return outputs.astype(jnp.bfloat16).reshape(TQ, D)
    attended = lax.map(per_question, (query_rows, passage_ids, live_slots))
    attended = attended.reshape(ROWS, D)
    return jnp.dot(attended, out_weight, preferred_element_type=jnp.float32).astype(jnp.bfloat16)
```

```python
import jax
import jax.numpy as jnp
from jax import lax
from jax.experimental import pallas as pl
from jax.experimental.pallas import tpu as pltpu
from jax.sharding import Mesh, PartitionSpec as P

DH = 64
P_SIZE = 64
TQ = 256
NEG = -1e30


def pack_kernel(pa_ref, k_ref, v_ref, out_ref):
    stored = k_ref.shape[0]

    def write(half):
        lo = half * DH
        for i in range(stored):
            key = k_ref[i, :, lo : lo + DH]
            value = v_ref[i, :, lo : lo + DH].astype(jnp.float32).T.astype(jnp.bfloat16)
            out_ref[0, i] = jnp.concatenate([key, value], axis=1)

    odd = lax.rem(pa_ref[0], 2)

    @pl.when(odd == 0)
    def _():
        write(0)

    @pl.when(odd == 1)
    def _():
        write(1)


def pack_heads(corpus_kv, pa, n_pa, n_y):
    stored, tokens, width2 = corpus_kv.shape
    value_block = width2 // 2 // 128
    per_y = n_pa * DH // 128
    return pl.pallas_call(
        pack_kernel,
        grid_spec=pltpu.PrefetchScalarGridSpec(
            num_scalar_prefetch=1,
            grid=(n_y,),
            in_specs=[
                pl.BlockSpec((stored, tokens, 128), lambda y, pa: (0, 0, y * per_y + pa[0] // 2)),
                pl.BlockSpec(
                    (stored, tokens, 128),
                    lambda y, pa: (0, 0, value_block + y * per_y + pa[0] // 2),
                ),
            ],
            out_specs=pl.BlockSpec((1, stored, tokens, 128), lambda y, pa: (y, 0, 0, 0)),
        ),
        out_shape=jax.ShapeDtypeStruct((n_y, stored, tokens, 128), jnp.bfloat16),
        name="pack_heads",
    )(pa, corpus_kv, corpus_kv)


def query_kernel(hidden_ref, gain_ref, weight_ref, out_ref, normed_ref):
    @pl.when(pl.program_id(0) == 0)
    def _():
        widened = hidden_ref[...].astype(jnp.float32)
        factor = lax.rsqrt(jnp.mean(widened * widened, axis=-1, keepdims=True) + 1e-06)
        normed_ref[...] = (widened * factor * gain_ref[...]).astype(jnp.bfloat16)

    product = jnp.dot(normed_ref[...], weight_ref[...], preferred_element_type=jnp.float32)
    out_ref[...] = product.T.astype(jnp.bfloat16)


def project_queries(hidden, gain, weight):
    rows, width = hidden.shape
    tile = 256
    return pl.pallas_call(
        query_kernel,
        grid=(width // tile,),
        in_specs=[
            pl.BlockSpec((rows, width), lambda i: (0, 0)),
            pl.BlockSpec((1, width), lambda i: (0, 0)),
            pl.BlockSpec((width, tile), lambda i: (0, i)),
        ],
        out_specs=pl.BlockSpec((tile, rows), lambda i: (i, 0)),
        out_shape=jax.ShapeDtypeStruct((width, rows), jnp.bfloat16),
        scratch_shapes=[pltpu.VMEM((rows, width), jnp.bfloat16)],
        compiler_params=pltpu.CompilerParams(vmem_limit_bytes=24 * 2**20),
        name="project_queries",
    )(hidden, gain.reshape(1, width), weight)


def attend_kernel(ids_ref, q_ref, kv_ref, out_ref, score_ref, n_pa, slots_dev):
    questions = q_ref.shape[0]
    slots = n_pa * slots_dev
    group = 4
    lane = lax.broadcasted_iota(jnp.int32, (P_SIZE, 2 * DH), 1)
    pad_row = lax.broadcasted_iota(jnp.int32, (DH, TQ), 0)
    pad = jnp.where(pad_row == 0, 1.0, 0.0).astype(jnp.bfloat16)

    def question(i, carry):
        y, j = i // n_pa, lax.rem(i, n_pa)
        count = ids_ref[y * n_pa, n_pa * slots_dev + j]
        queries = jnp.concatenate([q_ref[i], pad], axis=0)

        def passage(s):
            return ids_ref[y * n_pa + s // slots_dev, j * slots_dev + s % slots_dev]

        def run(parts):
            top = None
            for c in range(parts):
                rows = []
                for s in range(c * group, (c + 1) * group):
                    block = kv_ref[passage(s)]
                    bias = jnp.where(s < count, 0.0, NEG).astype(jnp.bfloat16)
                    rows.append(jnp.where(lane < DH, block, bias))
                scores = jnp.dot(
                    jnp.concatenate(rows, axis=0), queries, preferred_element_type=jnp.float32
                )
                score_ref[c] = scores
                highest = jnp.max(scores.reshape(-1, 8, TQ), axis=0)
                top = highest if top is None else jnp.maximum(top, highest)
            top = jnp.max(top, axis=0, keepdims=True)
            total = jnp.zeros((8, TQ), jnp.float32)
            number = jnp.zeros((DH, TQ), jnp.float32)
            for c in range(parts):
                weights = jnp.exp(score_ref[c] - top)
                total = total + jnp.sum(weights.reshape(-1, 8, TQ), axis=0)
                pairs = []
                for s in range(c * group, (c + 1) * group, 2):
                    first = pltpu.roll(kv_ref[passage(s)], DH, 1)
                    pairs.append(jnp.where(lane < DH, first, kv_ref[passage(s + 1)]))
                number = number + jnp.dot(
                    jnp.concatenate(pairs, axis=1),
                    weights.astype(jnp.bfloat16),
                    preferred_element_type=jnp.float32,
                )
            total = jnp.sum(total, axis=0, keepdims=True)
            out_ref[i] = (number / total).astype(jnp.bfloat16)

        needed = (count + group - 1) // group
        for parts in range(1, slots // group + 1):
            pl.when(needed == parts)(lambda parts=parts: run(parts))
        return carry

    lax.fori_loop(0, questions, question, 0)


def attend(ids, queries, kv, n_pa, slots_dev):
    questions = queries.shape[0]
    passages = kv.shape[0]
    return pl.pallas_call(
        lambda *refs: attend_kernel(*refs, n_pa=n_pa, slots_dev=slots_dev),
        grid_spec=pltpu.PrefetchScalarGridSpec(
            num_scalar_prefetch=1,
            grid=(1,),
            in_specs=[
                pl.BlockSpec((questions, DH, TQ), lambda i, ids: (0, 0, 0)),
                pl.BlockSpec((passages, P_SIZE, 2 * DH), lambda i, ids: (0, 0, 0)),
            ],
            out_specs=pl.BlockSpec((questions, DH, TQ), lambda i, ids: (0, 0, 0)),
            scratch_shapes=[pltpu.VMEM((n_pa * slots_dev // 4, 4 * P_SIZE, TQ), jnp.float32)],
        ),
        out_shape=jax.ShapeDtypeStruct((questions, DH, TQ), jnp.bfloat16),
        compiler_params=pltpu.CompilerParams(vmem_limit_bytes=24 * 2**20),
        name="attend",
    )(ids, queries, kv)


def output_kernel(att_ref, weight_ref, out_ref, rows_ref):
    @pl.when(pl.program_id(0) == 0)
    def _():
        for i in range(0, att_ref.shape[0], TQ):
            part = att_ref[i : i + TQ, :].astype(jnp.float32)
            rows_ref[:, i : i + TQ] = part.T.astype(jnp.bfloat16)

    out_ref[...] = jnp.dot(
        rows_ref[...], weight_ref[...], preferred_element_type=jnp.float32
    ).astype(jnp.bfloat16)


def project_output(attended, weight):
    width, rows = attended.shape
    tile = 256
    return pl.pallas_call(
        output_kernel,
        grid=(width // tile,),
        in_specs=[
            pl.BlockSpec((width, rows), lambda i: (0, 0)),
            pl.BlockSpec((width, tile), lambda i: (0, i)),
        ],
        out_specs=pl.BlockSpec((rows, tile), lambda i: (0, i)),
        out_shape=jax.ShapeDtypeStruct((rows, width), jnp.bfloat16),
        scratch_shapes=[pltpu.VMEM((rows, width), jnp.bfloat16)],
        compiler_params=pltpu.CompilerParams(vmem_limit_bytes=24 * 2**20),
        name="project_output",
    )(attended, weight)


def body(hidden_in, norm_gain, query_weight, out_weight, corpus_kv, owner_ids, local_ids, counts):
    n_y, n_pa = lax.axis_size("y"), lax.axis_size("pa")
    plane = ("y", "pa")
    width = hidden_in.shape[1]
    stored = corpus_kv.shape[0]
    slots_dev = owner_ids.shape[3]
    wanted = (owner_ids[..., 0] * stored + local_ids).reshape(-1)
    ids = lax.all_gather(jnp.concatenate([wanted, counts]), plane, axis=0)
    pa = lax.axis_index("pa").astype(jnp.int32).reshape(1)
    packed = pack_heads(corpus_kv, pa, n_pa, n_y)
    n_z = lax.axis_size("z")
    copies = jnp.broadcast_to(packed[None], (n_z,) + packed.shape).reshape((-1,) + packed.shape[1:])
    kv = lax.all_to_all(copies, ("z", "y"), 0, 0, tiled=True).reshape(-1, P_SIZE, 2 * DH)
    queries = project_queries(hidden_in, norm_gain, query_weight)
    queries = queries.reshape(width // DH, DH, TQ)
    queries = lax.all_to_all(queries, plane, 0, 0, tiled=True)
    attended = attend(ids, queries, kv, n_pa, slots_dev)
    attended = lax.all_to_all(attended, plane, 0, 0, tiled=True)
    return project_output(attended.reshape(width, TQ), out_weight)


def solution(mesh):
    split = Mesh(mesh.devices.reshape(4, 4, 8), ("z", "y", "pa"))
    pb = ("z", "y")
    every = ("z", "y", "pa")
    placed = (
        P(every, None),
        P(),
        P(),
        P(),
        P(pb, None, None),
        P(pb, "pa", None, None, None),
        P(pb, "pa", None, None),
        P(pb),
    )
    return jax.shard_map(
        body, mesh=split, in_specs=placed, out_specs=P(every, None), check_vma=False
    )
```

```python
import functools

import jax
import jax.numpy as jnp
from jax import lax
from jax.experimental import pallas as pl
from jax.experimental.pallas import tpu as pltpu
from jax.sharding import Mesh, PartitionSpec as P

DH = 64
P_SIZE = 64
TQ = 256
NEG = -1e30
EXTRA = 8
GROUP = 4
SIDE = 4
HEAD_AXES = ("zl", "y", "x")
OWNER_AXES = ("zh", "zl", "y")
EVERY = ("zh", "zl", "y", "x", "c")
LIMIT = 60 * 2**20


def whole():
    return pl.BlockSpec(memory_space=pltpu.VMEM)


def anywhere():
    return pl.BlockSpec(memory_space=pl.ANY)


def pack_kernel(corpus_ref, out_ref, key_ref, value_ref, sems, *, n_x):
    x, core = lax.axis_index("x"), lax.axis_index("c")
    n_far, n_near, half = out_ref.shape[:3]
    width = corpus_ref.shape[2] // 2
    copies = []
    for i in range(n_near):
        column = pl.multiple_of((i * n_x + x) // 2 * 128, 128)
        for n, (held, offset) in enumerate(((key_ref, 0), (value_ref, width))):
            copies.append(
                pltpu.make_async_copy(
                    corpus_ref.at[pl.ds(core * half, half), :, pl.ds(column + offset, 128)],
                    held.at[i],
                    sems.at[i, n],
                )
            )
    for copy in copies:
        copy.start()
    odd = lax.rem(x, 2) == 1
    lane = lax.broadcasted_iota(jnp.int32, (P_SIZE, 2 * DH), 1)
    for i in range(n_near):
        copies[2 * i].wait()
        copies[2 * i + 1].wait()
        for s in range(0, half, 2):
            both = value_ref[i, s : s + 2].reshape(2 * P_SIZE, 2 * DH).astype(jnp.float32).T
            mine = jnp.where(odd, both[DH:], both[:DH]).astype(jnp.bfloat16)
            for n, value in enumerate((pltpu.roll(mine, DH, 1), mine)):
                key = key_ref[i, s + n]
                key = jnp.where(odd, pltpu.roll(key, DH, 1), key)
                entry = jnp.where(lane < DH, key, value)
                for far in range(n_far):
                    out_ref[far, i, s + n] = entry


def pack_heads(corpus_kv, n_far, n_near, n_x):
    stored = corpus_kv.shape[0]
    block = (stored // 2, P_SIZE, 2 * DH)
    return pl.pallas_call(
        functools.partial(pack_kernel, n_x=n_x),
        in_specs=[anywhere()],
        out_specs=whole(),
        out_shape=jax.ShapeDtypeStruct((n_far, n_near) + block, jnp.bfloat16),
        scratch_shapes=[
            pltpu.VMEM((n_near,) + block, jnp.bfloat16),
            pltpu.VMEM((n_near,) + block, jnp.bfloat16),
            pltpu.SemaphoreType.DMA((n_near, 2)),
        ],
        compiler_params=pltpu.CompilerParams(vmem_limit_bytes=LIMIT),
        name="pack_heads",
    )(corpus_kv)


def fetch(weight_ref, held_ref, sems, chunk):
    copies = []
    for n in range(weight_ref.shape[0] // chunk):
        rows = pl.ds(n * chunk, chunk)
        copies.append(pltpu.make_async_copy(weight_ref.at[rows, :], held_ref.at[rows, :], sems.at[n]))
        copies[-1].start()
    return copies


def query_kernel(hidden_ref, gain_ref, extra_ref, weight_ref, out_ref, normed_ref, held_ref, sum_ref, sems):
    rows, width = hidden_ref.shape
    copies = fetch(weight_ref, held_ref, sems, TQ)
    for r in range(0, rows, 64):
        widened = hidden_ref[r : r + 64, :].astype(jnp.float32)
        factor = lax.rsqrt(jnp.mean(widened * widened, axis=-1, keepdims=True) + 1e-06)
        normed_ref[r : r + 64, :] = (widened * factor * gain_ref[...]).astype(jnp.bfloat16)
    for h in range(width // DH):
        out_ref[h, DH:, :] = extra_ref[...]
    for n, copy in enumerate(copies):
        copy.wait()
        depth = slice(n * TQ, (n + 1) * TQ)
        for s in range(0, width, TQ):
            columns = slice(s, s + TQ)
            product = jnp.dot(
                normed_ref[:, depth], held_ref[depth, columns], preferred_element_type=jnp.float32
            )
            if n > 0:
                product = product + sum_ref[:, columns]
            if n < len(copies) - 1:
                sum_ref[:, columns] = product
            else:
                turned = product.T.astype(jnp.bfloat16)
                for h in range(TQ // DH):
                    out_ref[s // DH + h, :DH, :] = turned[h * DH : (h + 1) * DH]


def projection_scratch(rows, width):
    return [
        pltpu.VMEM((rows, width), jnp.bfloat16),
        pltpu.VMEM((width, width), jnp.bfloat16),
        pltpu.VMEM((rows, width), jnp.float32),
        pltpu.SemaphoreType.DMA((width // TQ,)),
    ]


def project_queries(hidden, gain, extra, weight):
    rows, width = hidden.shape
    return pl.pallas_call(
        query_kernel,
        in_specs=[whole(), whole(), whole(), anywhere()],
        out_specs=whole(),
        out_shape=jax.ShapeDtypeStruct((width // DH, DH + EXTRA, rows), jnp.bfloat16),
        scratch_shapes=projection_scratch(rows, width),
        compiler_params=pltpu.CompilerParams(vmem_limit_bytes=LIMIT),
        name="project_queries",
    )(hidden, gain.reshape(1, width), extra, weight)


def output_kernel(attended_ref, weight_ref, out_ref, held_ref, sum_ref, sems):
    width = weight_ref.shape[1]
    copies = fetch(weight_ref, held_ref, sems, TQ)
    for n, copy in enumerate(copies):
        depth = slice(n * TQ, (n + 1) * TQ)
        rows = attended_ref[depth, :].astype(jnp.float32).T.astype(jnp.bfloat16)
        copy.wait()
        for s in range(0, width, TQ):
            columns = slice(s, s + TQ)
            product = jnp.dot(rows, held_ref[depth, columns], preferred_element_type=jnp.float32)
            if n > 0:
                product = product + sum_ref[:, columns]
            if n < len(copies) - 1:
                sum_ref[:, columns] = product
            else:
                out_ref[:, columns] = product.astype(jnp.bfloat16)


def project_output(attended, weight):
    width, rows = attended.shape
    return pl.pallas_call(
        output_kernel,
        in_specs=[whole(), anywhere()],
        out_specs=whole(),
        out_shape=jax.ShapeDtypeStruct((rows, width), jnp.bfloat16),
        scratch_shapes=projection_scratch(rows, width)[1:],
        compiler_params=pltpu.CompilerParams(vmem_limit_bytes=LIMIT),
        name="project_output",
    )(attended, weight)


def attend_kernel(ids_ref, q_ref, mine_ref, other_ref, out_ref, kv_ref, order_ref, sems, *score_refs, n_x):
    core = lax.axis_index("c")
    questions = q_ref.shape[0]
    half = mine_ref.shape[0]
    slots = n_x * 4
    most = slots // GROUP
    copies = [
        pltpu.make_async_copy(ref, kv_ref.at[pl.ds(n * half, half)], sems.at[n])
        for n, ref in enumerate((mine_ref, other_ref))
    ]
    for copy in copies:
        copy.start()
    lane = lax.broadcasted_iota(jnp.int32, (P_SIZE, 2 * DH), 1)
    pad_row = lax.broadcasted_iota(jnp.int32, (DH, TQ), 0)
    pad = jnp.where(pad_row == 0, 1.0, 0.0).astype(jnp.bfloat16)

    def number_in_group(i):
        return lax.rem(i, n_x) * 2 + core

    def count_of(i):
        return ids_ref[i, n_x * 8 + number_in_group(i)]

    def parts_of(i):
        return (count_of(i) + GROUP - 1) // GROUP

    def passage(i, s):
        return ids_ref[
            i // n_x * n_x + s // 4, s // 2 % 2 * n_x * 4 + number_in_group(i) * 2 + s % 2
        ]

    def place(i, at, want):
        order_ref[at] = i
        return at + (parts_of(i) == want).astype(jnp.int32)

    at = jnp.int32(0)
    for want in range(1, most + 1):
        at = lax.fori_loop(0, questions, functools.partial(place, want=want), at)
    for copy in copies:
        copy.wait()

    def run(parts, first):
        chosen = [order_ref[first + g] for g in range(SIDE)]
        tops = []
        for g, i in enumerate(chosen):
            count = count_of(i)
            queries = jnp.concatenate([q_ref[i, :DH, :], pad], axis=0)
            top = None
            for c in range(parts):
                rows = []
                for s in range(c * GROUP, (c + 1) * GROUP):
                    bias = jnp.where(s < count, 0.0, NEG).astype(jnp.bfloat16)
                    rows.append(jnp.where(lane < DH, kv_ref[passage(i, s)], bias))
                scores = jnp.dot(
                    jnp.concatenate(rows, axis=0), queries, preferred_element_type=jnp.float32
                )
                score_refs[g][c] = scores
                highest = jnp.max(scores.reshape(-1, 8, TQ), axis=0)
                top = highest if top is None else jnp.maximum(top, highest)
            tops.append(jnp.max(top, axis=0, keepdims=True))
        for g, i in enumerate(chosen):
            total = jnp.zeros((8, TQ), jnp.float32)
            number = jnp.zeros((DH, TQ), jnp.float32)
            for c in range(parts):
                weights = jnp.exp(score_refs[g][c] - tops[g])
                total = total + jnp.sum(weights.reshape(-1, 8, TQ), axis=0)
                pairs = []
                for s in range(c * GROUP, (c + 1) * GROUP, 2):
                    one = pltpu.roll(kv_ref[passage(i, s)], DH, 1)
                    pairs.append(jnp.where(lane < DH, one, kv_ref[passage(i, s + 1)]))
                number = number + jnp.dot(
                    jnp.concatenate(pairs, axis=1),
                    weights.astype(jnp.bfloat16),
                    preferred_element_type=jnp.float32,
                )
            total = jnp.sum(total, axis=0, keepdims=True)
            out_ref[i] = (number / total).astype(jnp.bfloat16)

    def several(t, carry):
        first = t * SIDE
        needed = parts_of(order_ref[first + SIDE - 1])
        for parts in range(1, most + 1):
            pl.when(needed == parts)(functools.partial(run, parts, first))
        return carry

    lax.fori_loop(0, questions // SIDE, several, 0)


def attend(ids, queries, mine, other, n_x):
    questions = queries.shape[0]
    half = mine.shape[0]
    return pl.pallas_call(
        functools.partial(attend_kernel, n_x=n_x),
        in_specs=[pl.BlockSpec(memory_space=pltpu.SMEM), whole(), anywhere(), anywhere()],
        out_specs=whole(),
        out_shape=jax.ShapeDtypeStruct((questions, DH, TQ), jnp.bfloat16),
        scratch_shapes=[
            pltpu.VMEM((2 * half, P_SIZE, 2 * DH), jnp.bfloat16),
            pltpu.SMEM((questions + 1,), jnp.int32),
            pltpu.SemaphoreType.DMA((2,)),
        ]
        + [pltpu.VMEM((n_x * 4 // GROUP, GROUP * P_SIZE, TQ), jnp.float32)] * SIDE,
        compiler_params=pltpu.CompilerParams(vmem_limit_bytes=LIMIT),
        name="attend",
    )(ids, queries, mine, other)


def swap_cores(value):
    return lax.ppermute(value, "c", [(0, 1), (1, 0)])


def body(hidden_in, norm_gain, query_weight, out_weight, corpus_kv, owner_ids, local_ids, counts):
    n_far, n_near, n_x = lax.axis_size("zh"), lax.axis_size("zl") * lax.axis_size("y"), lax.axis_size("x")
    core = lax.axis_index("c")
    width = hidden_in.shape[1]
    stored = corpus_kv.shape[0]
    wanted = (owner_ids[..., 0] * stored + local_ids).reshape(-1)
    swapped = swap_cores(wanted)
    first, second = jnp.where(core == 0, wanted, swapped), jnp.where(core == 0, swapped, wanted)
    table = jnp.concatenate([first, second, counts]).astype(jnp.bfloat16)
    entries = table.shape[0]
    extra = jnp.broadcast_to(jnp.pad(table, (0, TQ - entries))[None], (EXTRA, TQ))

    packed = pack_heads(corpus_kv, n_far, n_near, n_x)
    packed = packed.reshape((n_far * n_near,) + packed.shape[2:])
    mine = lax.all_to_all(packed, OWNER_AXES, 0, 0, tiled=True).reshape(-1, P_SIZE, 2 * DH)
    other = swap_cores(mine)

    queries = project_queries(hidden_in, norm_gain, extra, query_weight)
    queries = lax.all_to_all(queries, HEAD_AXES, 0, 0, tiled=True)
    ids = queries[:, DH, :entries].astype(jnp.int32)
    half = stored // 2
    local = ids % stored
    place = (local // half ^ core) * (mine.shape[0]) + ids // stored * half + local % half
    ids = jnp.where(jnp.arange(entries)[None, :] < 2 * wanted.shape[0], place, ids)

    attended = attend(ids, queries, mine, other, n_x)
    attended = lax.all_to_all(attended, HEAD_AXES, 0, 0, tiled=True)
    return project_output(attended.reshape(width, TQ), out_weight)


def solution(mesh):
    split = Mesh(mesh.devices.reshape(2, 2, 4, 4, 2), EVERY)
    owner, inner = OWNER_AXES, ("x", "c")
    placed = (
        P(EVERY, None),
        P(),
        P(),
        P(),
        P(owner, None, None),
        P(owner, inner, None, None, None),
        P(owner, inner, None, None),
        P(owner),
    )
    return jax.shard_map(
        body, mesh=split, in_specs=placed, out_specs=P(EVERY, None), check_vma=False
    )
```

```python
import functools

import jax
import jax.numpy as jnp
from jax import lax
from jax.experimental import pallas as pl
from jax.experimental.pallas import tpu as pltpu
from jax.sharding import Mesh, PartitionSpec as P

DH = 64
P_SIZE = 64
TQ = 256
NEG = -1e30
EXTRA = 8
GROUP = 4
SIDE = 4
HEAD_AXES = ("zl", "y", "x")
NEAR_AXES = ("zl", "y")
OWNER_AXES = ("zh", "zl", "y")
EVERY = ("zh", "zl", "y", "x", "c")
LIMIT = 60 * 2**20


def whole():
    return pl.BlockSpec(memory_space=pltpu.VMEM)


def anywhere():
    return pl.BlockSpec(memory_space=pl.ANY)


def turned(i, count, far):
    return lax.rem(i + count // 2 * far, count)


def pack_kernel(corpus_ref, out_ref, key_ref, value_ref, sems, *, n_x):
    x, core, far = lax.axis_index("x"), lax.axis_index("c"), lax.axis_index("zh")
    n_near, half = out_ref.shape[:2]
    width = corpus_ref.shape[2] // 2
    copies = []
    for i in range(n_near):
        column = pl.multiple_of((turned(i, n_near, far) * n_x + x) // 2 * 128, 128)
        for n, (held, offset) in enumerate(((key_ref, 0), (value_ref, width))):
            copies.append(
                pltpu.make_async_copy(
                    corpus_ref.at[pl.ds(core * half, half), :, pl.ds(column + offset, 128)],
                    held.at[i],
                    sems.at[i, n],
                )
            )
    for copy in copies:
        copy.start()
    odd = lax.rem(x, 2) == 1
    lane = lax.broadcasted_iota(jnp.int32, (P_SIZE, 2 * DH), 1)
    for i in range(n_near):
        copies[2 * i].wait()
        copies[2 * i + 1].wait()
        for s in range(0, half, 2):
            both = value_ref[i, s : s + 2].reshape(2 * P_SIZE, 2 * DH).astype(jnp.float32).T
            mine = jnp.where(odd, both[DH:], both[:DH]).astype(jnp.bfloat16)
            for n, value in enumerate((pltpu.roll(mine, DH, 1), mine)):
                key = key_ref[i, s + n]
                key = jnp.where(odd, pltpu.roll(key, DH, 1), key)
                out_ref[i, s + n] = jnp.where(lane < DH, key, value)


def pack_heads(corpus_kv, n_near, n_x):
    stored = corpus_kv.shape[0]
    block = (stored // 2, P_SIZE, 2 * DH)
    return pl.pallas_call(
        functools.partial(pack_kernel, n_x=n_x),
        in_specs=[anywhere()],
        out_specs=whole(),
        out_shape=jax.ShapeDtypeStruct((n_near,) + block, jnp.bfloat16),
        scratch_shapes=[
            pltpu.VMEM((n_near,) + block, jnp.bfloat16),
            pltpu.VMEM((n_near,) + block, jnp.bfloat16),
            pltpu.SemaphoreType.DMA((n_near, 2)),
        ],
        compiler_params=pltpu.CompilerParams(vmem_limit_bytes=LIMIT),
        name="pack_heads",
    )(corpus_kv)


def fetch(weight_ref, held_ref, sems, chunk_of):
    copies = []
    for n in range(weight_ref.shape[0] // TQ):
        rows = pl.ds(pl.multiple_of(chunk_of(n) * TQ, TQ), TQ)
        copies.append(
            pltpu.make_async_copy(
                weight_ref.at[rows, :], held_ref.at[pl.ds(n * TQ, TQ), :], sems.at[n]
            )
        )
        copies[-1].start()
    return copies


def query_kernel(hidden_ref, gain_ref, extra_ref, weight_ref, out_ref, normed_ref, held_ref, sum_ref, sems):
    rows, width = hidden_ref.shape
    far = lax.axis_index("zh")
    copies = fetch(weight_ref, held_ref, sems, lambda n: n)
    for r in range(0, rows, 64):
        widened = hidden_ref[r : r + 64, :].astype(jnp.float32)
        factor = lax.rsqrt(jnp.mean(widened * widened, axis=-1, keepdims=True) + 1e-06)
        normed_ref[r : r + 64, :] = (widened * factor * gain_ref[...]).astype(jnp.bfloat16)
    for h in range(width // DH):
        out_ref[h, DH:, :] = extra_ref[...]
    for n, copy in enumerate(copies):
        copy.wait()
        depth = slice(n * TQ, (n + 1) * TQ)
        for s in range(0, width, TQ):
            columns = slice(s, s + TQ)
            product = jnp.dot(
                normed_ref[:, depth], held_ref[depth, columns], preferred_element_type=jnp.float32
            )
            if n > 0:
                product = product + sum_ref[:, columns]
            if n < len(copies) - 1:
                sum_ref[:, columns] = product
            else:
                by_head = product.T.astype(jnp.bfloat16)
                for h in range(TQ // DH):
                    place = turned(s // DH + h, width // DH, far)
                    out_ref[place, :DH, :] = by_head[h * DH : (h + 1) * DH]


def projection_scratch(rows, width):
    return [
        pltpu.VMEM((rows, width), jnp.bfloat16),
        pltpu.VMEM((width, width), jnp.bfloat16),
        pltpu.VMEM((rows, width), jnp.float32),
        pltpu.SemaphoreType.DMA((width // TQ,)),
    ]


def project_queries(hidden, gain, extra, weight):
    rows, width = hidden.shape
    return pl.pallas_call(
        query_kernel,
        in_specs=[whole(), whole(), whole(), anywhere()],
        out_specs=whole(),
        out_shape=jax.ShapeDtypeStruct((width // DH, DH + EXTRA, rows), jnp.bfloat16),
        scratch_shapes=projection_scratch(rows, width),
        compiler_params=pltpu.CompilerParams(vmem_limit_bytes=LIMIT),
        name="project_queries",
    )(hidden, gain.reshape(1, width), extra, weight)


def output_kernel(attended_ref, weight_ref, out_ref, held_ref, sum_ref, sems):
    width = weight_ref.shape[1]
    far = lax.axis_index("zh")
    copies = fetch(weight_ref, held_ref, sems, lambda n: turned(n, width // TQ, far))
    for n, copy in enumerate(copies):
        depth = slice(n * TQ, (n + 1) * TQ)
        rows = attended_ref[depth, :].astype(jnp.float32).T.astype(jnp.bfloat16)
        copy.wait()
        for s in range(0, width, TQ):
            columns = slice(s, s + TQ)
            product = jnp.dot(rows, held_ref[depth, columns], preferred_element_type=jnp.float32)
            if n > 0:
                product = product + sum_ref[:, columns]
            if n < len(copies) - 1:
                sum_ref[:, columns] = product
            else:
                out_ref[:, columns] = product.astype(jnp.bfloat16)


def project_output(attended, weight):
    width, rows = attended.shape
    return pl.pallas_call(
        output_kernel,
        in_specs=[whole(), anywhere()],
        out_specs=whole(),
        out_shape=jax.ShapeDtypeStruct((rows, width), jnp.bfloat16),
        scratch_shapes=projection_scratch(rows, width)[1:],
        compiler_params=pltpu.CompilerParams(vmem_limit_bytes=LIMIT),
        name="project_output",
    )(attended, weight)


def attend_kernel(ids_ref, q_ref, *refs, n_x):
    part_refs, (out_ref, kv_ref, order_ref, sems), score_refs = refs[:4], refs[4:8], refs[8:]
    core = lax.axis_index("c")
    questions = q_ref.shape[0]
    size = part_refs[0].shape[0]
    slots = n_x * 4
    most = slots // GROUP
    copies = [
        pltpu.make_async_copy(ref, kv_ref.at[pl.ds(n * size, size)], sems.at[n])
        for n, ref in enumerate(part_refs)
    ]
    for copy in copies:
        copy.start()
    lane = lax.broadcasted_iota(jnp.int32, (P_SIZE, 2 * DH), 1)
    pad_row = lax.broadcasted_iota(jnp.int32, (DH, TQ), 0)
    pad = jnp.where(pad_row == 0, 1.0, 0.0).astype(jnp.bfloat16)

    def number_in_group(i):
        return lax.rem(i, n_x) * 2 + core

    def count_of(i):
        return ids_ref[i, n_x * 8 + number_in_group(i)]

    def parts_of(i):
        return (count_of(i) + GROUP - 1) // GROUP

    def passage(i, s):
        return ids_ref[
            i // n_x * n_x + s // 4, s // 2 % 2 * n_x * 4 + number_in_group(i) * 2 + s % 2
        ]

    def place(i, at, want):
        order_ref[at] = i
        return at + (parts_of(i) == want).astype(jnp.int32)

    at = jnp.int32(0)
    for want in range(1, most + 1):
        at = lax.fori_loop(0, questions, functools.partial(place, want=want), at)
    for copy in copies:
        copy.wait()

    def run(parts, first):
        chosen = [order_ref[first + g] for g in range(SIDE)]
        tops = []
        for g, i in enumerate(chosen):
            count = count_of(i)
            queries = jnp.concatenate([q_ref[i, :DH, :], pad], axis=0)
            top = None
            for c in range(parts):
                rows = []
                for s in range(c * GROUP, (c + 1) * GROUP):
                    bias = jnp.where(s < count, 0.0, NEG).astype(jnp.bfloat16)
                    rows.append(jnp.where(lane < DH, kv_ref[passage(i, s)], bias))
                scores = jnp.dot(
                    jnp.concatenate(rows, axis=0), queries, preferred_element_type=jnp.float32
                )
                score_refs[g][c] = scores
                highest = jnp.max(scores.reshape(-1, 8, TQ), axis=0)
                top = highest if top is None else jnp.maximum(top, highest)
            tops.append(jnp.max(top, axis=0, keepdims=True))
        for g, i in enumerate(chosen):
            total = jnp.zeros((8, TQ), jnp.float32)
            number = jnp.zeros((DH, TQ), jnp.float32)
            for c in range(parts):
                weights = jnp.exp(score_refs[g][c] - tops[g])
                total = total + jnp.sum(weights.reshape(-1, 8, TQ), axis=0)
                pairs = []
                for s in range(c * GROUP, (c + 1) * GROUP, 2):
                    one = pltpu.roll(kv_ref[passage(i, s)], DH, 1)
                    pairs.append(jnp.where(lane < DH, one, kv_ref[passage(i, s + 1)]))
                number = number + jnp.dot(
                    jnp.concatenate(pairs, axis=1),
                    weights.astype(jnp.bfloat16),
                    preferred_element_type=jnp.float32,
                )
            total = jnp.sum(total, axis=0, keepdims=True)
            out_ref[i] = (number / total).astype(jnp.bfloat16)

    def several(t, carry):
        first = t * SIDE
        needed = parts_of(order_ref[first + SIDE - 1])
        for parts in range(1, most + 1):
            pl.when(needed == parts)(functools.partial(run, parts, first))
        return carry

    lax.fori_loop(0, questions // SIDE, several, 0)


def attend(ids, queries, parts, n_x):
    questions = queries.shape[0]
    size = parts[0].shape[0]
    return pl.pallas_call(
        functools.partial(attend_kernel, n_x=n_x),
        in_specs=[pl.BlockSpec(memory_space=pltpu.SMEM), whole()] + [whole()] * len(parts),
        out_specs=whole(),
        out_shape=jax.ShapeDtypeStruct((questions, DH, TQ), jnp.bfloat16),
        scratch_shapes=[
            pltpu.VMEM((len(parts) * size, P_SIZE, 2 * DH), jnp.bfloat16),
            pltpu.SMEM((questions + 1,), jnp.int32),
            pltpu.SemaphoreType.DMA((len(parts),)),
        ]
        + [pltpu.VMEM((n_x * 4 // GROUP, GROUP * P_SIZE, TQ), jnp.float32)] * SIDE,
        compiler_params=pltpu.CompilerParams(vmem_limit_bytes=20 * 2**20),
        name="attend",
    )(ids, queries, *parts)


def swap_cores(value):
    return lax.ppermute(value, "c", [(0, 1), (1, 0)])


def body(hidden_in, norm_gain, query_weight, out_weight, corpus_kv, owner_ids, local_ids, counts):
    n_near, n_x = lax.axis_size("zl") * lax.axis_size("y"), lax.axis_size("x")
    far_index, core = lax.axis_index("zh"), lax.axis_index("c")
    width = hidden_in.shape[1]
    stored = corpus_kv.shape[0]
    wanted = (owner_ids[..., 0] * stored + local_ids).reshape(-1)
    swapped = swap_cores(wanted)
    first, second = jnp.where(core == 0, wanted, swapped), jnp.where(core == 0, swapped, wanted)
    table = jnp.concatenate([first, second, counts]).astype(jnp.bfloat16)
    entries = table.shape[0]
    extra = jnp.broadcast_to(jnp.pad(table, (0, TQ - entries))[None], (EXTRA, TQ))

    packed = pack_heads(corpus_kv, n_near, n_x)
    near = lax.all_to_all(packed, NEAR_AXES, 0, 0, tiled=True).reshape(-1, P_SIZE, 2 * DH)
    far = lax.ppermute(near, ("zh", "zl"), [(0, 3), (3, 0), (1, 2), (2, 1)])
    parts = (near, swap_cores(near), far, swap_cores(far))

    queries = project_queries(hidden_in, norm_gain, extra, query_weight)
    queries = lax.all_to_all(queries, HEAD_AXES, 0, 0, tiled=True)
    ids = queries[:, DH, :entries].astype(jnp.int32)
    half = stored // 2
    owner, local = ids // stored, ids % stored
    part = (owner // n_near ^ far_index) * 2 + (local // half ^ core)
    place = (part * n_near + owner % n_near) * half + local % half
    ids = jnp.where(jnp.arange(entries)[None, :] < 2 * wanted.shape[0], place, ids)

    attended = attend(ids, queries, parts, n_x)
    attended = lax.all_to_all(attended, HEAD_AXES, 0, 0, tiled=True)
    return project_output(attended.reshape(width, TQ), out_weight)


def solution(mesh):
    split = Mesh(mesh.devices.reshape(2, 2, 4, 4, 2), EVERY)
    owner, inner = OWNER_AXES, ("x", "c")
    placed = (
        P(EVERY, None),
        P(),
        P(),
        P(),
        P(owner, None, None),
        P(owner, inner, None, None, None),
        P(owner, inner, None, None),
        P(owner),
    )
    return jax.shard_map(
        body, mesh=split, in_specs=placed, out_specs=P(EVERY, None), check_vma=False
    )
```

```python
import functools

import jax
import jax.numpy as jnp
from jax import lax
from jax.experimental import pallas as pl
from jax.experimental.pallas import tpu as pltpu
from jax.sharding import Mesh, PartitionSpec as P

DH = 64
P_SIZE = 64
TQ = 256
NEG = -1e30
EXTRA = 8
GROUP = 4
SIDE = 8
HEAD_AXES = ("zl", "y", "x")
NEAR_AXES = ("zl", "y")
OWNER_AXES = ("zh", "zl", "y")
EVERY = ("zh", "zl", "y", "x", "c")
LIMIT = 60 * 2**20


def whole():
    return pl.BlockSpec(memory_space=pltpu.VMEM)


def anywhere():
    return pl.BlockSpec(memory_space=pl.ANY)


def turned(i, count, far):
    return lax.rem(i + count // 2 * far, count)


def pack_kernel(corpus_ref, out_ref, key_ref, value_ref, sems, *, n_x):
    x, core, far = lax.axis_index("x"), lax.axis_index("c"), lax.axis_index("zh")
    n_near, half = out_ref.shape[:2]
    width = corpus_ref.shape[2] // 2
    copies = []
    for i in range(n_near):
        column = pl.multiple_of((turned(i, n_near, far) * n_x + x) // 2 * 128, 128)
        for n, (held, offset) in enumerate(((key_ref, 0), (value_ref, width))):
            copies.append(
                pltpu.make_async_copy(
                    corpus_ref.at[pl.ds(core * half, half), :, pl.ds(column + offset, 128)],
                    held.at[i],
                    sems.at[i, n],
                )
            )
    for copy in copies:
        copy.start()
    odd = lax.rem(x, 2) == 1
    lane = lax.broadcasted_iota(jnp.int32, (P_SIZE, 2 * DH), 1)
    for copy in copies:
        copy.wait()
    for i in range(n_near):
        for s in range(0, half, 2):
            both = value_ref[i, s : s + 2].reshape(2 * P_SIZE, 2 * DH).T
            mine = jnp.where(odd, both[DH:], both[:DH])
            for n, value in enumerate((pltpu.roll(mine, DH, 1), mine)):
                key = key_ref[i, s + n]
                key = jnp.where(odd, pltpu.roll(key, DH, 1), key)
                out_ref[i, s + n] = jnp.where(lane < DH, key, value)


def pack_heads(corpus_kv, n_near, n_x):
    stored = corpus_kv.shape[0]
    block = (stored // 2, P_SIZE, 2 * DH)
    return pl.pallas_call(
        functools.partial(pack_kernel, n_x=n_x),
        in_specs=[anywhere()],
        out_specs=whole(),
        out_shape=jax.ShapeDtypeStruct((n_near,) + block, jnp.bfloat16),
        scratch_shapes=[
            pltpu.VMEM((n_near,) + block, jnp.bfloat16),
            pltpu.VMEM((n_near,) + block, jnp.bfloat16),
            pltpu.SemaphoreType.DMA((n_near, 2)),
        ],
        compiler_params=pltpu.CompilerParams(vmem_limit_bytes=LIMIT),
        name="pack_heads",
    )(corpus_kv)


def fetch(weight_ref, held_ref, sems, chunk_of):
    copies = []
    for n in range(weight_ref.shape[0] // TQ):
        rows = pl.ds(pl.multiple_of(chunk_of(n) * TQ, TQ), TQ)
        copies.append(
            pltpu.make_async_copy(
                weight_ref.at[rows, :], held_ref.at[pl.ds(n * TQ, TQ), :], sems.at[n]
            )
        )
        copies[-1].start()
    return copies


def query_kernel(hidden_ref, gain_ref, extra_ref, weight_ref, out_ref, normed_ref, held_ref, sum_ref, sems):
    rows, width = hidden_ref.shape
    far = lax.axis_index("zh")
    copies = fetch(weight_ref, held_ref, sems, lambda n: n)
    for r in range(0, rows, 64):
        widened = hidden_ref[r : r + 64, :].astype(jnp.float32)
        factor = lax.rsqrt(jnp.mean(widened * widened, axis=-1, keepdims=True) + 1e-06)
        normed_ref[r : r + 64, :] = (widened * factor * gain_ref[...]).astype(jnp.bfloat16)
    for h in range(width // DH):
        out_ref[h, DH:, :] = extra_ref[...]
    for n, copy in enumerate(copies):
        copy.wait()
        depth = slice(n * TQ, (n + 1) * TQ)
        for s in range(0, width, TQ):
            columns = slice(s, s + TQ)
            product = jnp.dot(
                normed_ref[:, depth], held_ref[depth, columns], preferred_element_type=jnp.float32
            )
            if n > 0:
                product = product + sum_ref[:, columns]
            if n < len(copies) - 1:
                sum_ref[:, columns] = product
            else:
                by_head = product.T.astype(jnp.bfloat16)
                for h in range(TQ // DH):
                    place = turned(s // DH + h, width // DH, far)
                    out_ref[place, :DH, :] = by_head[h * DH : (h + 1) * DH]


def projection_scratch(rows, width):
    return [
        pltpu.VMEM((rows, width), jnp.bfloat16),
        pltpu.VMEM((width, width), jnp.bfloat16),
        pltpu.VMEM((rows, width), jnp.float32),
        pltpu.SemaphoreType.DMA((width // TQ,)),
    ]


def project_queries(hidden, gain, extra, weight):
    rows, width = hidden.shape
    return pl.pallas_call(
        query_kernel,
        in_specs=[whole(), whole(), whole(), anywhere()],
        out_specs=whole(),
        out_shape=jax.ShapeDtypeStruct((width // DH, DH + EXTRA, rows), jnp.bfloat16),
        scratch_shapes=projection_scratch(rows, width),
        compiler_params=pltpu.CompilerParams(vmem_limit_bytes=LIMIT),
        name="project_queries",
    )(hidden, gain.reshape(1, width), extra, weight)


def output_kernel(attended_ref, weight_ref, out_ref, rows_ref):
    width = weight_ref.shape[1]
    for n in range(0, width, TQ):
        rows_ref[:, n : n + TQ] = attended_ref[n : n + TQ, :].T
    for n in range(0, width, TQ):
        columns = slice(n, n + TQ)
        out_ref[:, columns] = jnp.dot(
            rows_ref[...], weight_ref[:, columns], preferred_element_type=jnp.float32
        ).astype(jnp.bfloat16)


def project_output(attended, weight):
    width, rows = attended.shape
    return pl.pallas_call(
        output_kernel,
        in_specs=[whole(), whole()],
        out_specs=whole(),
        out_shape=jax.ShapeDtypeStruct((rows, width), jnp.bfloat16),
        scratch_shapes=[pltpu.VMEM((rows, width), jnp.bfloat16)],
        compiler_params=pltpu.CompilerParams(vmem_limit_bytes=16 * 2**20),
        name="project_output",
    )(attended, pltpu.with_memory_space_constraint(weight, pltpu.VMEM))


def attend_kernel(ids_ref, q_ref, *refs, n_x):
    part_refs, weight_ref, (out_ref, held_ref), refs = refs[:4], refs[4], refs[5:7], refs[7:]
    (kv_ref, order_ref, sems, weight_sems), score_refs = refs[:4], refs[4:]
    core, far = lax.axis_index("c"), lax.axis_index("zh")
    questions = q_ref.shape[0]
    size = part_refs[0].shape[0]
    slots = n_x * 4
    most = slots // GROUP
    copies = [
        pltpu.make_async_copy(ref, kv_ref.at[pl.ds(n * size, size)], sems.at[n])
        for n, ref in enumerate(part_refs)
    ]
    for copy in copies:
        copy.start()
    chunks = weight_ref.shape[0] // TQ
    weights_in = fetch(weight_ref, held_ref, weight_sems, lambda n: turned(n, chunks, far))
    lane = lax.broadcasted_iota(jnp.int32, (P_SIZE, 2 * DH), 1)
    pad_row = lax.broadcasted_iota(jnp.int32, (DH, TQ), 0)
    pad = jnp.where(pad_row == 0, 1.0, 0.0).astype(jnp.bfloat16)

    def number_in_group(i):
        return i % n_x * 2 + core

    def count_of(i):
        return ids_ref[i, n_x * 8 + number_in_group(i)]

    def parts_of(i):
        return (count_of(i) + GROUP - 1) // GROUP

    def passage(i, s):
        return ids_ref[
            i // n_x * n_x + s // 4, s // 2 % 2 * n_x * 4 + number_in_group(i) * 2 + s % 2
        ]

    needs = [parts_of(i) for i in range(questions)]
    at = jnp.int32(0)
    for want in range(1, most + 1):
        for i in range(questions):
            order_ref[at] = i
            at = at + jnp.where(needs[i] == want, 1, 0)
    for copy in copies:
        copy.wait()

    def run(parts, first):
        chosen = [order_ref[first + g] for g in range(SIDE)]
        tops = []
        for g, i in enumerate(chosen):
            count = count_of(i)
            queries = jnp.concatenate([q_ref[i, :DH, :], pad], axis=0)
            top = None
            for c in range(parts):
                rows = []
                for s in range(c * GROUP, (c + 1) * GROUP):
                    bias = jnp.where(s < count, 0.0, NEG).astype(jnp.bfloat16)
                    rows.append(jnp.where(lane < DH, kv_ref[passage(i, s)], bias))
                scores = jnp.dot(
                    jnp.concatenate(rows, axis=0), queries, preferred_element_type=jnp.float32
                )
                score_refs[g][c] = scores
                highest = jnp.max(scores.reshape(-1, 8, TQ), axis=0)
                top = highest if top is None else jnp.maximum(top, highest)
            tops.append(jnp.max(top, axis=0, keepdims=True))
        for g, i in enumerate(chosen):
            total = jnp.zeros((8, TQ), jnp.float32)
            number = jnp.zeros((DH, TQ), jnp.float32)
            for c in range(parts):
                weights = jnp.exp(score_refs[g][c] - tops[g])
                total = total + jnp.sum(weights.reshape(-1, 8, TQ), axis=0)
                pairs = []
                for s in range(c * GROUP, (c + 1) * GROUP, 2):
                    one = pltpu.roll(kv_ref[passage(i, s)], DH, 1)
                    pairs.append(jnp.where(lane < DH, one, kv_ref[passage(i, s + 1)]))
                number = number + jnp.dot(
                    jnp.concatenate(pairs, axis=1),
                    weights.astype(jnp.bfloat16),
                    preferred_element_type=jnp.float32,
                )
            total = jnp.sum(total, axis=0, keepdims=True)
            out_ref[i] = (number / total).astype(jnp.bfloat16)

    def several(t, carry):
        first = t * SIDE
        needed = parts_of(order_ref[first + SIDE - 1])
        for parts in range(1, most + 1):
            pl.when(needed == parts)(functools.partial(run, parts, first))
        return carry

    lax.fori_loop(0, questions // SIDE, several, 0)
    for copy in weights_in:
        copy.wait()


def attend(ids, queries, parts, weight, n_x):
    questions = queries.shape[0]
    size = parts[0].shape[0]
    return pl.pallas_call(
        functools.partial(attend_kernel, n_x=n_x),
        in_specs=[pl.BlockSpec(memory_space=pltpu.SMEM), whole()] + [whole()] * len(parts) + [pl.BlockSpec(memory_space=pltpu.HBM)],
        out_specs=(whole(), whole()),
        out_shape=(
            jax.ShapeDtypeStruct((questions, DH, TQ), jnp.bfloat16),
            pltpu.VMEM(weight.shape, jnp.bfloat16),
        ),
        scratch_shapes=[
            pltpu.VMEM((len(parts) * size, P_SIZE, 2 * DH), jnp.bfloat16),
            pltpu.SMEM((questions + 1,), jnp.int32),
            pltpu.SemaphoreType.DMA((len(parts),)),
            pltpu.SemaphoreType.DMA((weight.shape[0] // TQ,)),
        ]
        + [pltpu.VMEM((n_x * 4 // GROUP, GROUP * P_SIZE, TQ), jnp.float32)] * SIDE,
        compiler_params=pltpu.CompilerParams(vmem_limit_bytes=32 * 2**20),
        name="attend",
    )(ids, queries, *parts, pltpu.with_memory_space_constraint(weight, pltpu.HBM))


def swap_cores(value):
    return lax.ppermute(value, "c", [(0, 1), (1, 0)])


def body(hidden_in, norm_gain, query_weight, out_weight, corpus_kv, owner_ids, local_ids, counts):
    n_near, n_x = lax.axis_size("zl") * lax.axis_size("y"), lax.axis_size("x")
    far_index, core = lax.axis_index("zh"), lax.axis_index("c")
    width = hidden_in.shape[1]
    stored = corpus_kv.shape[0]
    wanted = (owner_ids[..., 0] * stored + local_ids).reshape(-1)
    swapped = swap_cores(wanted)
    first, second = jnp.where(core == 0, wanted, swapped), jnp.where(core == 0, swapped, wanted)
    table = jnp.concatenate([first, second, counts]).astype(jnp.bfloat16)
    entries = table.shape[0]
    extra = jnp.broadcast_to(jnp.pad(table, (0, TQ - entries))[None], (EXTRA, TQ))

    packed = pack_heads(corpus_kv, n_near, n_x)
    near = lax.all_to_all(packed, NEAR_AXES, 0, 0, tiled=True).reshape(-1, P_SIZE, 2 * DH)
    far = lax.ppermute(near, ("zh", "zl"), [(0, 3), (3, 0), (1, 2), (2, 1)])
    parts = (near, swap_cores(near), far, swap_cores(far))

    queries = project_queries(hidden_in, norm_gain, extra, query_weight)
    queries = lax.all_to_all(queries, HEAD_AXES, 0, 0, tiled=True)
    ids = queries[:, DH, :entries].astype(jnp.int32)
    half = stored // 2
    owner, local = ids // stored, ids % stored
    part = (owner // n_near ^ far_index) * 2 + (local // half ^ core)
    place = (part * n_near + owner % n_near) * half + local % half
    ids = jnp.where(jnp.arange(entries)[None, :] < 2 * wanted.shape[0], place, ids)

    attended, weight = attend(ids, queries, parts, out_weight, n_x)
    attended = lax.all_to_all(attended, HEAD_AXES, 0, 0, tiled=True)
    return project_output(attended.reshape(width, TQ), weight)


def solution(mesh):
    split = Mesh(mesh.devices.reshape(2, 2, 4, 4, 2), EVERY)
    owner, inner = OWNER_AXES, ("x", "c")
    placed = (
        P(EVERY, None),
        P(),
        P(),
        P(),
        P(owner, None, None),
        P(owner, inner, None, None, None),
        P(owner, inner, None, None),
        P(owner),
    )
    return jax.shard_map(
        body, mesh=split, in_specs=placed, out_specs=P(EVERY, None), check_vma=False
    )
```

```python
import functools

import jax
import jax.numpy as jnp
from jax import lax
from jax.experimental import pallas as pl
from jax.experimental.pallas import tpu as pltpu
from jax.sharding import Mesh, PartitionSpec as P

DH = 64
P_SIZE = 64
TQ = 256
TILE = 512
NEG = -1e30
EXTRA = 8
GROUP = 4
SIDE = 8
HEAD_AXES = ("zl", "y", "x")
NEAR_AXES = ("zl", "y")
OWNER_AXES = ("zh", "zl", "y")
EVERY = ("zh", "zl", "y", "x", "c")
LIMIT = 60 * 2**20


def whole():
    return pl.BlockSpec(memory_space=pltpu.VMEM)


def anywhere():
    return pl.BlockSpec(memory_space=pl.ANY)


def turned(i, count, far):
    return lax.rem(i + count // 2 * far, count)


def pack_kernel(corpus_ref, out_ref, key_ref, value_ref, sems, *, n_x):
    x, core, far = lax.axis_index("x"), lax.axis_index("c"), lax.axis_index("zh")
    n_near, half = out_ref.shape[:2]
    width = corpus_ref.shape[2] // 2
    copies = []
    for i in range(n_near):
        column = pl.multiple_of((turned(i, n_near, far) * n_x + x) // 2 * 128, 128)
        for n, (held, offset) in enumerate(((key_ref, 0), (value_ref, width))):
            copies.append(
                pltpu.make_async_copy(
                    corpus_ref.at[pl.ds(core * half, half), :, pl.ds(column + offset, 128)],
                    held.at[i],
                    sems.at[i, n],
                )
            )
    for copy in copies:
        copy.start()
    odd = lax.rem(x, 2) == 1
    lane = lax.broadcasted_iota(jnp.int32, (P_SIZE, 2 * DH), 1)
    for copy in copies:
        copy.wait()
    for i in range(n_near):
        for s in range(0, half, 2):
            both = value_ref[i, s : s + 2].reshape(2 * P_SIZE, 2 * DH).T
            mine = jnp.where(odd, both[DH:], both[:DH])
            for n, value in enumerate((pltpu.roll(mine, DH, 1), mine)):
                key = key_ref[i, s + n]
                key = jnp.where(odd, pltpu.roll(key, DH, 1), key)
                out_ref[i, s + n] = jnp.where(lane < DH, key, value)


def pack_heads(corpus_kv, n_near, n_x):
    stored = corpus_kv.shape[0]
    block = (stored // 2, P_SIZE, 2 * DH)
    return pl.pallas_call(
        functools.partial(pack_kernel, n_x=n_x),
        in_specs=[pl.BlockSpec(memory_space=pltpu.HBM)],
        out_specs=whole(),
        out_shape=pltpu.VMEM((n_near,) + block, jnp.bfloat16),
        scratch_shapes=[
            pltpu.VMEM((n_near,) + block, jnp.bfloat16),
            pltpu.VMEM((n_near,) + block, jnp.bfloat16),
            pltpu.SemaphoreType.DMA((n_near, 2)),
        ],
        compiler_params=pltpu.CompilerParams(vmem_limit_bytes=16 * 2**20),
        name="pack_heads",
    )(pltpu.with_memory_space_constraint(corpus_kv, pltpu.HBM))


def fetch(weight_ref, held_ref, sems, chunk_of):
    copies = []
    for n in range(weight_ref.shape[0] // TQ):
        rows = pl.ds(pl.multiple_of(chunk_of(n) * TQ, TQ), TQ)
        copies.append(
            pltpu.make_async_copy(
                weight_ref.at[rows, :], held_ref.at[pl.ds(n * TQ, TQ), :], sems.at[n]
            )
        )
        copies[-1].start()
    return copies


def query_kernel(hidden_ref, gain_ref, extra_ref, weight_ref, out_ref, normed_ref, held_ref, sum_ref, sems):
    rows, width = hidden_ref.shape
    far = lax.axis_index("zh")
    copies = fetch(weight_ref, held_ref, sems, lambda n: n)
    for r in range(0, rows, 64):
        widened = hidden_ref[r : r + 64, :].astype(jnp.float32)
        factor = lax.rsqrt(jnp.mean(widened * widened, axis=-1, keepdims=True) + 1e-06)
        normed_ref[r : r + 64, :] = (widened * factor * gain_ref[...]).astype(jnp.bfloat16)
    for h in range(width // DH):
        out_ref[h, DH:, :] = extra_ref[...]
    for n, copy in enumerate(copies):
        copy.wait()
        depth = slice(n * TQ, (n + 1) * TQ)
        for s in range(0, width, TQ):
            columns = slice(s, s + TQ)
            product = jnp.dot(
                normed_ref[:, depth], held_ref[depth, columns], preferred_element_type=jnp.float32
            )
            if n > 0:
                product = product + sum_ref[:, columns]
            if n < len(copies) - 1:
                sum_ref[:, columns] = product
            else:
                by_head = product.T.astype(jnp.bfloat16)
                for h in range(TQ // DH):
                    place = turned(s // DH + h, width // DH, far)
                    out_ref[place, :DH, :] = by_head[h * DH : (h + 1) * DH]


def projection_scratch(rows, width):
    return [
        pltpu.VMEM((rows, width), jnp.bfloat16),
        pltpu.VMEM((width, width), jnp.bfloat16),
        pltpu.VMEM((rows, width), jnp.float32),
        pltpu.SemaphoreType.DMA((width // TQ,)),
    ]


def project_queries(hidden, gain, extra, weight):
    rows, width = hidden.shape
    return pl.pallas_call(
        query_kernel,
        in_specs=[whole(), whole(), whole(), pl.BlockSpec(memory_space=pltpu.HBM)],
        out_specs=whole(),
        out_shape=pltpu.VMEM((width // DH, DH + EXTRA, rows), jnp.bfloat16),
        scratch_shapes=projection_scratch(rows, width),
        compiler_params=pltpu.CompilerParams(vmem_limit_bytes=32 * 2**20),
        name="project_queries",
    )(hidden, gain.reshape(1, width), extra, pltpu.with_memory_space_constraint(weight, pltpu.HBM))


def output_kernel(attended_ref, weight_ref, out_ref, rows_ref, tile_ref, sems):
    width = weight_ref.shape[1]
    copies = []
    for n in range(0, width, TQ):
        rows_ref[:, n : n + TQ] = attended_ref[n : n + TQ, :].T
    for n in range(width // TILE):
        columns = slice(n * TILE, (n + 1) * TILE)
        tile_ref[n] = jnp.dot(
            rows_ref[...], weight_ref[:, columns], preferred_element_type=jnp.float32
        ).astype(jnp.bfloat16)
        copies.append(
            pltpu.make_async_copy(tile_ref.at[n], out_ref.at[:, pl.ds(n * TILE, TILE)], sems.at[n])
        )
        copies[-1].start()
    for copy in copies:
        copy.wait()


def project_output(attended, weight):
    width, rows = attended.shape
    return pl.pallas_call(
        output_kernel,
        in_specs=[whole(), whole()],
        out_specs=pl.BlockSpec(memory_space=pltpu.HBM),
        out_shape=jax.ShapeDtypeStruct((rows, width), jnp.bfloat16),
        scratch_shapes=[
            pltpu.VMEM((rows, width), jnp.bfloat16),
            pltpu.VMEM((width // TILE, rows, TILE), jnp.bfloat16),
            pltpu.SemaphoreType.DMA((width // TILE,)),
        ],
        compiler_params=pltpu.CompilerParams(vmem_limit_bytes=16 * 2**20),
        name="project_output",
    )(attended, pltpu.with_memory_space_constraint(weight, pltpu.VMEM))


def attend_kernel(ids_ref, q_ref, *refs, n_x):
    part_refs, weight_ref, (out_ref, held_ref), refs = refs[:4], refs[4], refs[5:7], refs[7:]
    (kv_ref, order_ref, sems, weight_sems), score_refs = refs[:4], refs[4:]
    core, far = lax.axis_index("c"), lax.axis_index("zh")
    questions = q_ref.shape[0]
    size = part_refs[0].shape[0]
    slots = n_x * 4
    most = slots // GROUP
    copies = [
        pltpu.make_async_copy(ref, kv_ref.at[pl.ds(n * size, size)], sems.at[n])
        for n, ref in enumerate(part_refs)
    ]
    for copy in copies:
        copy.start()
    chunks = weight_ref.shape[0] // TQ
    weights_in = fetch(weight_ref, held_ref, weight_sems, lambda n: turned(n, chunks, far))
    lane = lax.broadcasted_iota(jnp.int32, (P_SIZE, 2 * DH), 1)
    pad_row = lax.broadcasted_iota(jnp.int32, (DH, TQ), 0)
    pad = jnp.where(pad_row == 0, 1.0, 0.0).astype(jnp.bfloat16)

    def number_in_group(i):
        return i % n_x * 2 + core

    def count_of(i):
        return ids_ref[i, n_x * 8 + number_in_group(i)]

    def parts_of(i):
        return (count_of(i) + GROUP - 1) // GROUP

    def passage(i, s):
        return ids_ref[
            i // n_x * n_x + s // 4, s // 2 % 2 * n_x * 4 + number_in_group(i) * 2 + s % 2
        ]

    needs = [parts_of(i) for i in range(questions)]
    at = jnp.int32(0)
    for want in range(1, most + 1):
        for i in range(questions):
            order_ref[at] = i
            at = at + jnp.where(needs[i] == want, 1, 0)
    for copy in copies:
        copy.wait()

    def run(parts, first):
        chosen = [order_ref[first + g] for g in range(SIDE)]
        tops = []
        for g, i in enumerate(chosen):
            count = count_of(i)
            queries = jnp.concatenate([q_ref[i, :DH, :], pad], axis=0)
            top = None
            for c in range(parts):
                rows = []
                for s in range(c * GROUP, (c + 1) * GROUP):
                    bias = jnp.where(s < count, 0.0, NEG).astype(jnp.bfloat16)
                    rows.append(jnp.where(lane < DH, kv_ref[passage(i, s)], bias))
                scores = jnp.dot(
                    jnp.concatenate(rows, axis=0), queries, preferred_element_type=jnp.float32
                )
                score_refs[g][c] = scores
                highest = jnp.max(scores.reshape(-1, 8, TQ), axis=0)
                top = highest if top is None else jnp.maximum(top, highest)
            tops.append(jnp.max(top, axis=0, keepdims=True))
        for g, i in enumerate(chosen):
            total = jnp.zeros((8, TQ), jnp.float32)
            number = jnp.zeros((DH, TQ), jnp.float32)
            for c in range(parts):
                weights = jnp.exp(score_refs[g][c] - tops[g])
                total = total + jnp.sum(weights.reshape(-1, 8, TQ), axis=0)
                pairs = []
                for s in range(c * GROUP, (c + 1) * GROUP, 2):
                    one = pltpu.roll(kv_ref[passage(i, s)], DH, 1)
                    pairs.append(jnp.where(lane < DH, one, kv_ref[passage(i, s + 1)]))
                number = number + jnp.dot(
                    jnp.concatenate(pairs, axis=1),
                    weights.astype(jnp.bfloat16),
                    preferred_element_type=jnp.float32,
                )
            total = jnp.sum(total, axis=0, keepdims=True)
            out_ref[i] = (number / total).astype(jnp.bfloat16)

    def several(t, carry):
        first = t * SIDE
        needed = parts_of(order_ref[first + SIDE - 1])
        for parts in range(1, most + 1):
            pl.when(needed == parts)(functools.partial(run, parts, first))
        return carry

    lax.fori_loop(0, questions // SIDE, several, 0)
    for copy in weights_in:
        copy.wait()


def attend(ids, queries, parts, weight, n_x):
    questions = queries.shape[0]
    size = parts[0].shape[0]
    return pl.pallas_call(
        functools.partial(attend_kernel, n_x=n_x),
        in_specs=[pl.BlockSpec(memory_space=pltpu.SMEM), whole()] + [whole()] * len(parts) + [pl.BlockSpec(memory_space=pltpu.HBM)],
        out_specs=(whole(), whole()),
        out_shape=(
            jax.ShapeDtypeStruct((questions, DH, TQ), jnp.bfloat16),
            pltpu.VMEM(weight.shape, jnp.bfloat16),
        ),
        scratch_shapes=[
            pltpu.VMEM((len(parts) * size, P_SIZE, 2 * DH), jnp.bfloat16),
            pltpu.SMEM((questions + 1,), jnp.int32),
            pltpu.SemaphoreType.DMA((len(parts),)),
            pltpu.SemaphoreType.DMA((weight.shape[0] // TQ,)),
        ]
        + [pltpu.VMEM((n_x * 4 // GROUP, GROUP * P_SIZE, TQ), jnp.float32)] * SIDE,
        compiler_params=pltpu.CompilerParams(vmem_limit_bytes=32 * 2**20),
        name="attend",
    )(ids, queries, *parts, pltpu.with_memory_space_constraint(weight, pltpu.HBM))


def swap_cores(value):
    return lax.ppermute(value, "c", [(0, 1), (1, 0)])


def body(hidden_in, norm_gain, query_weight, out_weight, corpus_kv, owner_ids, local_ids, counts):
    n_near, n_x = lax.axis_size("zl") * lax.axis_size("y"), lax.axis_size("x")
    far_index, core = lax.axis_index("zh"), lax.axis_index("c")
    width = hidden_in.shape[1]
    stored = corpus_kv.shape[0]
    wanted = (owner_ids[..., 0] * stored + local_ids).reshape(-1)
    swapped = swap_cores(wanted)
    first, second = jnp.where(core == 0, wanted, swapped), jnp.where(core == 0, swapped, wanted)
    table = jnp.concatenate([first, second, counts]).astype(jnp.bfloat16)
    entries = table.shape[0]
    extra = jnp.broadcast_to(jnp.pad(table, (0, TQ - entries))[None], (EXTRA, TQ))

    packed = pack_heads(corpus_kv, n_near, n_x)
    near = lax.all_to_all(packed, NEAR_AXES, 0, 0, tiled=True).reshape(-1, P_SIZE, 2 * DH)
    far = lax.ppermute(near, ("zh", "zl"), [(0, 3), (3, 0), (1, 2), (2, 1)])
    parts = (near, swap_cores(near), far, swap_cores(far))

    queries = project_queries(hidden_in, norm_gain, extra, query_weight)
    queries = lax.all_to_all(queries, HEAD_AXES, 0, 0, tiled=True)
    ids = queries[:, DH, :entries].astype(jnp.int32)
    half = stored // 2
    owner, local = ids // stored, ids % stored
    part = (owner // n_near ^ far_index) * 2 + (local // half ^ core)
    place = (part * n_near + owner % n_near) * half + local % half
    ids = jnp.where(jnp.arange(entries)[None, :] < 2 * wanted.shape[0], place, ids)

    attended, weight = attend(ids, queries, parts, out_weight, n_x)
    attended = lax.all_to_all(attended, HEAD_AXES, 0, 0, tiled=True)
    return project_output(attended.reshape(width, TQ), weight)


def solution(mesh):
    split = Mesh(mesh.devices.reshape(2, 2, 4, 4, 2), EVERY)
    owner, inner = OWNER_AXES, ("x", "c")
    placed = (
        P(EVERY, None),
        P(),
        P(),
        P(),
        P(owner, None, None),
        P(owner, inner, None, None, None),
        P(owner, inner, None, None),
        P(owner),
    )
    return jax.shard_map(
        body, mesh=split, in_specs=placed, out_specs=P(EVERY, None), check_vma=False
    )
```

```python
import functools

import jax
import jax.numpy as jnp
from jax import lax
from jax.experimental import pallas as pl
from jax.experimental.pallas import tpu as pltpu
from jax.sharding import Mesh, PartitionSpec as P

DH = 64
P_SIZE = 64
TQ = 256
TILE = 512
NEG = -1e30
EXTRA = 8
GROUP = 4
SIDE = 8
HEAD_AXES = ("zl", "y", "x")
NEAR_AXES = ("y", "zl")
OWNER_AXES = ("zh", "zl", "y")
EVERY = ("zh", "zl", "y", "x", "c")
LIMIT = 60 * 2**20


def whole():
    return pl.BlockSpec(memory_space=pltpu.VMEM)


def anywhere():
    return pl.BlockSpec(memory_space=pl.ANY)


def turned(i, count, far):
    return lax.rem(i + count // 2 * far, count)


def pack_kernel(corpus_ref, out_ref, key_ref, value_ref, sems, *, n_x):
    x, core, far = lax.axis_index("x"), lax.axis_index("c"), lax.axis_index("zh")
    n_near, half = out_ref.shape[:2]
    width = corpus_ref.shape[2] // 2
    copies = []
    for i in range(n_near):
        head = turned(i % 2 * (n_near // 2) + i // 2, n_near, far)
        column = pl.multiple_of((head * n_x + x) // 2 * 128, 128)
        for n, (held, offset) in enumerate(((key_ref, 0), (value_ref, width))):
            copies.append(
                pltpu.make_async_copy(
                    corpus_ref.at[pl.ds(core * half, half), :, pl.ds(column + offset, 128)],
                    held.at[i],
                    sems.at[i, n],
                )
            )
    for copy in copies:
        copy.start()
    odd = lax.rem(x, 2) == 1
    lane = lax.broadcasted_iota(jnp.int32, (P_SIZE, 2 * DH), 1)
    for copy in copies:
        copy.wait()
    for i in range(n_near):
        for s in range(0, half, 2):
            both = value_ref[i, s : s + 2].reshape(2 * P_SIZE, 2 * DH).T
            mine = jnp.where(odd, both[DH:], both[:DH])
            for n, value in enumerate((pltpu.roll(mine, DH, 1), mine)):
                key = key_ref[i, s + n]
                key = jnp.where(odd, pltpu.roll(key, DH, 1), key)
                out_ref[i, s + n] = jnp.where(lane < DH, key, value)


def pack_heads(corpus_kv, n_near, n_x):
    stored = corpus_kv.shape[0]
    block = (stored // 2, P_SIZE, 2 * DH)
    return pl.pallas_call(
        functools.partial(pack_kernel, n_x=n_x),
        in_specs=[pl.BlockSpec(memory_space=pltpu.HBM)],
        out_specs=whole(),
        out_shape=pltpu.VMEM((n_near,) + block, jnp.bfloat16),
        scratch_shapes=[
            pltpu.VMEM((n_near,) + block, jnp.bfloat16),
            pltpu.VMEM((n_near,) + block, jnp.bfloat16),
            pltpu.SemaphoreType.DMA((n_near, 2)),
        ],
        compiler_params=pltpu.CompilerParams(vmem_limit_bytes=16 * 2**20),
        name="pack_heads",
    )(pltpu.with_memory_space_constraint(corpus_kv, pltpu.HBM))


def fetch(weight_ref, held_ref, sems, chunk_of):
    copies = []
    for n in range(weight_ref.shape[0] // TQ):
        rows = pl.ds(pl.multiple_of(chunk_of(n) * TQ, TQ), TQ)
        copies.append(
            pltpu.make_async_copy(
                weight_ref.at[rows, :], held_ref.at[pl.ds(n * TQ, TQ), :], sems.at[n]
            )
        )
        copies[-1].start()
    return copies


def query_kernel(hidden_ref, gain_ref, extra_ref, weight_ref, out_ref, normed_ref, held_ref, sum_ref, sems):
    rows, width = hidden_ref.shape
    far = lax.axis_index("zh")
    copies = fetch(weight_ref, held_ref, sems, lambda n: n)
    for r in range(0, rows, 64):
        widened = hidden_ref[r : r + 64, :].astype(jnp.float32)
        factor = lax.rsqrt(jnp.mean(widened * widened, axis=-1, keepdims=True) + 1e-06)
        normed_ref[r : r + 64, :] = (widened * factor * gain_ref[...]).astype(jnp.bfloat16)
    for h in range(width // DH):
        out_ref[h, DH:, :] = extra_ref[...]
    for n, copy in enumerate(copies):
        copy.wait()
        depth = slice(n * TQ, (n + 1) * TQ)
        for s in range(0, width, TQ):
            columns = slice(s, s + TQ)
            product = jnp.dot(
                normed_ref[:, depth], held_ref[depth, columns], preferred_element_type=jnp.float32
            )
            if n > 0:
                product = product + sum_ref[:, columns]
            if n < len(copies) - 1:
                sum_ref[:, columns] = product
            else:
                by_head = product.T.astype(jnp.bfloat16)
                for h in range(TQ // DH):
                    place = turned(s // DH + h, width // DH, far)
                    out_ref[place, :DH, :] = by_head[h * DH : (h + 1) * DH]


def projection_scratch(rows, width):
    return [
        pltpu.VMEM((rows, width), jnp.bfloat16),
        pltpu.VMEM((width, width), jnp.bfloat16),
        pltpu.VMEM((rows, width), jnp.float32),
        pltpu.SemaphoreType.DMA((width // TQ,)),
    ]


def project_queries(hidden, gain, extra, weight):
    rows, width = hidden.shape
    return pl.pallas_call(
        query_kernel,
        in_specs=[whole(), whole(), whole(), pl.BlockSpec(memory_space=pltpu.HBM)],
        out_specs=whole(),
        out_shape=pltpu.VMEM((width // DH, DH + EXTRA, rows), jnp.bfloat16),
        scratch_shapes=projection_scratch(rows, width),
        compiler_params=pltpu.CompilerParams(vmem_limit_bytes=32 * 2**20),
        name="project_queries",
    )(hidden, gain.reshape(1, width), extra, pltpu.with_memory_space_constraint(weight, pltpu.HBM))


def output_kernel(attended_ref, weight_ref, out_ref, rows_ref, tile_ref, sems):
    width = weight_ref.shape[1]
    copies = []
    for n in range(0, width, TQ):
        rows_ref[:, n : n + TQ] = attended_ref[n : n + TQ, :].T
    for n in range(width // TILE):
        columns = slice(n * TILE, (n + 1) * TILE)
        tile_ref[n] = jnp.dot(
            rows_ref[...], weight_ref[:, columns], preferred_element_type=jnp.float32
        ).astype(jnp.bfloat16)
        copies.append(
            pltpu.make_async_copy(tile_ref.at[n], out_ref.at[:, pl.ds(n * TILE, TILE)], sems.at[n])
        )
        copies[-1].start()
    for copy in copies:
        copy.wait()


def project_output(attended, weight):
    width, rows = attended.shape
    return pl.pallas_call(
        output_kernel,
        in_specs=[whole(), whole()],
        out_specs=pl.BlockSpec(memory_space=pltpu.HBM),
        out_shape=jax.ShapeDtypeStruct((rows, width), jnp.bfloat16),
        scratch_shapes=[
            pltpu.VMEM((rows, width), jnp.bfloat16),
            pltpu.VMEM((width // TILE, rows, TILE), jnp.bfloat16),
            pltpu.SemaphoreType.DMA((width // TILE,)),
        ],
        compiler_params=pltpu.CompilerParams(vmem_limit_bytes=16 * 2**20),
        name="project_output",
    )(attended, pltpu.with_memory_space_constraint(weight, pltpu.VMEM))


def attend_kernel(ids_ref, q_ref, *refs, n_x):
    part_refs, weight_ref, (out_ref, held_ref), refs = refs[:4], refs[4], refs[5:7], refs[7:]
    (kv_ref, order_ref, sems, weight_sems), score_refs = refs[:4], refs[4:]
    core, far = lax.axis_index("c"), lax.axis_index("zh")
    questions = q_ref.shape[0]
    size = part_refs[0].shape[0]
    slots = n_x * 4
    most = slots // GROUP
    copies = [
        pltpu.make_async_copy(ref, kv_ref.at[pl.ds(n * size, size)], sems.at[n])
        for n, ref in enumerate(part_refs)
    ]
    for copy in copies:
        copy.start()
    chunks = weight_ref.shape[0] // TQ
    weights_in = fetch(weight_ref, held_ref, weight_sems, lambda n: turned(n, chunks, far))
    lane = lax.broadcasted_iota(jnp.int32, (P_SIZE, 2 * DH), 1)
    pad_row = lax.broadcasted_iota(jnp.int32, (DH, TQ), 0)
    pad = jnp.where(pad_row == 0, 1.0, 0.0).astype(jnp.bfloat16)

    def number_in_group(i):
        return i % n_x * 2 + core

    def count_of(i):
        return ids_ref[i, n_x * 8 + number_in_group(i)]

    def parts_of(i):
        return (count_of(i) + GROUP - 1) // GROUP

    def passage(i, s):
        return ids_ref[
            i // n_x * n_x + s // 4, s // 2 % 2 * n_x * 4 + number_in_group(i) * 2 + s % 2
        ]

    needs = [parts_of(i) for i in range(questions)]
    at = jnp.int32(0)
    for want in range(1, most + 1):
        for i in range(questions):
            order_ref[at] = i
            at = at + jnp.where(needs[i] == want, 1, 0)
    for copy in copies:
        copy.wait()

    def run(parts, first):
        chosen = [order_ref[first + g] for g in range(SIDE)]
        tops = []
        for g, i in enumerate(chosen):
            count = count_of(i)
            queries = jnp.concatenate([q_ref[i, :DH, :], pad], axis=0)
            top = None
            for c in range(parts):
                rows = []
                for s in range(c * GROUP, (c + 1) * GROUP):
                    bias = jnp.where(s < count, 0.0, NEG).astype(jnp.bfloat16)
                    rows.append(jnp.where(lane < DH, kv_ref[passage(i, s)], bias))
                scores = jnp.dot(
                    jnp.concatenate(rows, axis=0), queries, preferred_element_type=jnp.float32
                )
                score_refs[g][c] = scores
                highest = jnp.max(scores.reshape(-1, 8, TQ), axis=0)
                top = highest if top is None else jnp.maximum(top, highest)
            tops.append(jnp.max(top, axis=0, keepdims=True))
        for g, i in enumerate(chosen):
            total = jnp.zeros((8, TQ), jnp.float32)
            number = jnp.zeros((DH, TQ), jnp.float32)
            for c in range(parts):
                weights = jnp.exp(score_refs[g][c] - tops[g])
                total = total + jnp.sum(weights.reshape(-1, 8, TQ), axis=0)
                pairs = []
                for s in range(c * GROUP, (c + 1) * GROUP, 2):
                    one = pltpu.roll(kv_ref[passage(i, s)], DH, 1)
                    pairs.append(jnp.where(lane < DH, one, kv_ref[passage(i, s + 1)]))
                number = number + jnp.dot(
                    jnp.concatenate(pairs, axis=1),
                    weights.astype(jnp.bfloat16),
                    preferred_element_type=jnp.float32,
                )
            total = jnp.sum(total, axis=0, keepdims=True)
            out_ref[i] = (number / total).astype(jnp.bfloat16)

    def several(t, carry):
        first = t * SIDE
        needed = parts_of(order_ref[first + SIDE - 1])
        for parts in range(1, most + 1):
            pl.when(needed == parts)(functools.partial(run, parts, first))
        return carry

    lax.fori_loop(0, questions // SIDE, several, 0)
    for copy in weights_in:
        copy.wait()


def attend(ids, queries, parts, weight, n_x):
    questions = queries.shape[0]
    size = parts[0].shape[0]
    return pl.pallas_call(
        functools.partial(attend_kernel, n_x=n_x),
        in_specs=[pl.BlockSpec(memory_space=pltpu.SMEM), whole()] + [whole()] * len(parts) + [pl.BlockSpec(memory_space=pltpu.HBM)],
        out_specs=(whole(), whole()),
        out_shape=(
            jax.ShapeDtypeStruct((questions, DH, TQ), jnp.bfloat16),
            pltpu.VMEM(weight.shape, jnp.bfloat16),
        ),
        scratch_shapes=[
            pltpu.VMEM((len(parts) * size, P_SIZE, 2 * DH), jnp.bfloat16),
            pltpu.SMEM((questions + 1,), jnp.int32),
            pltpu.SemaphoreType.DMA((len(parts),)),
            pltpu.SemaphoreType.DMA((weight.shape[0] // TQ,)),
        ]
        + [pltpu.VMEM((n_x * 4 // GROUP, GROUP * P_SIZE, TQ), jnp.float32)] * SIDE,
        compiler_params=pltpu.CompilerParams(vmem_limit_bytes=32 * 2**20),
        name="attend",
    )(ids, queries, *parts, pltpu.with_memory_space_constraint(weight, pltpu.HBM))


def swap_cores(value):
    return lax.ppermute(value, "c", [(0, 1), (1, 0)])


def body(hidden_in, norm_gain, query_weight, out_weight, corpus_kv, owner_ids, local_ids, counts):
    n_near, n_x = lax.axis_size("zl") * lax.axis_size("y"), lax.axis_size("x")
    far_index, core = lax.axis_index("zh"), lax.axis_index("c")
    width = hidden_in.shape[1]
    stored = corpus_kv.shape[0]
    wanted = (owner_ids[..., 0] * stored + local_ids).reshape(-1)
    swapped = swap_cores(wanted)
    first, second = jnp.where(core == 0, wanted, swapped), jnp.where(core == 0, swapped, wanted)
    table = jnp.concatenate([first, second, counts]).astype(jnp.bfloat16)
    entries = table.shape[0]
    extra = jnp.broadcast_to(jnp.pad(table, (0, TQ - entries))[None], (EXTRA, TQ))

    packed = pack_heads(corpus_kv, n_near, n_x)
    near = lax.all_to_all(packed, NEAR_AXES, 0, 0, tiled=True).reshape(-1, P_SIZE, 2 * DH)
    far = lax.ppermute(near, ("zh", "zl"), [(0, 3), (3, 0), (1, 2), (2, 1)])
    parts = (near, swap_cores(near), far, swap_cores(far))

    queries = project_queries(hidden_in, norm_gain, extra, query_weight)
    queries = lax.all_to_all(queries, HEAD_AXES, 0, 0, tiled=True)
    ids = queries[:, DH, :entries].astype(jnp.int32)
    half = stored // 2
    owner, local = ids // stored, ids % stored
    part = (owner // n_near ^ far_index) * 2 + (local // half ^ core)
    near_place = owner % (n_near // 2) * 2 + owner % n_near // (n_near // 2)
    place = (part * n_near + near_place) * half + local % half
    ids = jnp.where(jnp.arange(entries)[None, :] < 2 * wanted.shape[0], place, ids)

    attended, weight = attend(ids, queries, parts, out_weight, n_x)
    attended = lax.all_to_all(attended, HEAD_AXES, 0, 0, tiled=True)
    return project_output(attended.reshape(width, TQ), weight)


def solution(mesh):
    split = Mesh(mesh.devices.reshape(2, 2, 4, 4, 2), EVERY)
    owner, inner = OWNER_AXES, ("x", "c")
    placed = (
        P(EVERY, None),
        P(),
        P(),
        P(),
        P(owner, None, None),
        P(owner, inner, None, None, None),
        P(owner, inner, None, None),
        P(owner),
    )
    return jax.shard_map(
        body, mesh=split, in_specs=placed, out_specs=P(EVERY, None), check_vma=False
    )
```
